512 devices in a mesh: depth: 8 (over z_lo), row: 8 (over y, core), col: 8 (over z_hi, x).
Axes of the slice: x: 4, y: 4, z: 16 (z_hi: 2, z_lo: 8; z = z_hi * 8 + z_lo), core: 2. Of those that a mesh axis runs over, the one named last changes fastest.
Arguments:
- tokens: bfloat16 [256, 12288], P(('depth', 'row'), 'col'), may hold values from -6 to 6
- w_up: bfloat16 [24576, 12288], P(('depth', 'row'), 'col'), may hold values from -0.0546875 to 0.0546875
- w_down: bfloat16 [24576, 12288], P(('depth', 'row'), 'col'), may hold values from -0.0390625 to 0.0390625
- grad_out: bfloat16 [256, 12288], P(('depth', 'row'), 'col'), may hold values from -6 to 6
Outputs:
- out: bfloat16 [256, 12288], P(('depth', 'row'), 'col')
- grad_in: bfloat16 [256, 12288], P(('depth', 'row'), 'col')
- grad_w_up: bfloat16 [24576, 12288], P(('depth', 'row'), 'col')
- grad_w_down: bfloat16 [24576, 12288], P(('depth', 'row'), 'col')
The draws below stay inside these ranges and needn't reach their ends.
All inputs are finite; a program needn't handle non-finite values.
Results may differ from the reference program's by a relative error of at most 0.024.
Values may be sent and summed in bfloat16 or wider, within the bound.
A program may use at most 64 MiB of HBM per device.

```python
import math
import jax
import jax.numpy as jnp
from jax import lax

D = 12288
FF = 24576
TOKENS = 256


def shard_levels(key, shape, cuts, least, top_value):
    loudness, own = 1.0, jax.random.fold_in(key, 6)
    for axis_at, shards_of in cuts:
        heights = jnp.exp(jax.random.uniform(jax.random.fold_in(own, axis_at), (shards_of,), jnp.float32, least / len(cuts), top_value / len(cuts)))
        loudness = loudness * jnp.repeat(heights, shape[axis_at] // shards_of).reshape([-1 if axis == axis_at else 1 for axis in range(len(shape))])
    return loudness


def bell_draw(key, shape, spread, bound, split=(), kind=jnp.bfloat16):
    loudness = shard_levels(key, shape, split, -0.22, 0.18) if split else 1.0
    entries = jax.random.normal(key, shape, jnp.float32) * spread * loudness
    return jnp.minimum(jnp.maximum(entries, -bound), bound).astype(kind)


def setup_inputs(seed: int = 0) -> dict:
    seeds = jax.random.split(jax.random.key(seed), 5)
    return {
        "tokens": bell_draw(seeds[0], (TOKENS, D), 1.0, 6.0, ((0, 64), (1, 8))),
        "w_up": bell_draw(seeds[1], (FF, D), D ** -0.5, 0.0546875, ((0, 64), (1, 8))),
        "w_down": bell_draw(seeds[2], (FF, D), FF ** -0.5, 0.0390625, ((0, 64), (1, 8))),
        "grad_out": bell_draw(seeds[3], (TOKENS, D), 1.0, 6.0, ((0, 64), (1, 8))),
    }


coeff = 0.7978845608028654

def gelu_value(value):
    inner = jnp.tanh(coeff * (value + 0.044715 * value * value * value))
    return 0.5 * value * (1.0 + inner)

def gelu_slope(value):
    inner = jnp.tanh(coeff * (value + 0.044715 * value * value * value))
    return 0.5 * (1.0 + inner) + 0.5 * value * (1.0 - inner * inner) * coeff * (1.0 + 3.0 * 0.044715 * value * value)

def reference(tokens, w_up, w_down, grad_out):
    scale = 1.0 / math.sqrt(TOKENS)
    pre = lax.dot_general(tokens, w_up, (((1,), (1,)), ((), ())), preferred_element_type=jnp.float32)
    act = gelu_value(pre).astype(jnp.bfloat16)
    out = jnp.dot(act, w_down, preferred_element_type=jnp.float32).astype(jnp.bfloat16)
    grad_act = lax.dot_general(grad_out, w_down, (((1,), (1,)), ((), ())), preferred_element_type=jnp.float32)
    grad_pre = (grad_act * gelu_slope(pre)).astype(jnp.bfloat16)
    grad_in = jnp.dot(grad_pre, w_up, preferred_element_type=jnp.float32).astype(jnp.bfloat16)
    grad_w_up = (lax.dot_general(grad_pre, tokens, (((0,), (0,)), ((), ())), preferred_element_type=jnp.float32) * scale).astype(jnp.bfloat16)
    grad_w_down = (lax.dot_general(act, grad_out, (((0,), (0,)), ((), ())), preferred_element_type=jnp.float32) * scale).astype(jnp.bfloat16)
    return (out, grad_in, grad_w_up, grad_w_down)
```

```python
import functools
import math

import jax
import jax.numpy as jnp
from jax import lax
from jax.experimental import pallas as pl
from jax.experimental.pallas import tpu as pltpu
from jax.sharding import PartitionSpec as P

MESH = pl.DeviceIdType.MESH
NX, NY, NZ = 4, 4, 8
F32, BF16 = jnp.float32, jnp.bfloat16
coeff = 0.7978845608028654


def gelu_value(value):
    inner = jnp.tanh(coeff * (value + 0.044715 * value * value * value))
    return 0.5 * value * (1.0 + inner)


def gelu_slope(value):
    inner = jnp.tanh(coeff * (value + 0.044715 * value * value * value))
    return 0.5 * (1.0 + inner) + 0.5 * value * (1.0 - inner * inner) * coeff * (
        1.0 + 3.0 * 0.044715 * value * value
    )


def along_rows(left, right):
    return lax.dot_general(left, right, (((1,), (1,)), ((), ())), preferred_element_type=F32)


def over_tokens(left, right):
    return lax.dot_general(left, right, (((0,), (0,)), ((), ())), preferred_element_type=F32)


def kernel(
    scale,
    tok_ref, w_up_ref, w_down_ref, grad_ref,
    out_ref, gin_ref, gwu_ref, gwd_ref,
    weights, wouts, pieces, full, part, xin, far_out, far_in, hidden,
    core_out, core_in, y_out, y_in, z_out, z_in, last_out, last_in,
    w_sem, o_sem, az, ay, ac, xr, fz, xa, rc, ry, rz, rl,
):
    depth, row, col = lax.axis_index("depth"), lax.axis_index("row"), lax.axis_index("col")
    z, y, core, x = depth, row // 2, row % 2, col % NX

    def at(z=depth, y=y, core=core, col=col):
        return {"depth": z, "row": y * 2 + core, "col": col}

    z_peers = [(z + k) % NZ for k in (4, 3, 5, 2, 6, 1, 7)]
    y_peers = [(y + k) % NY for k in (2, 1, 3)]
    x_peers = [(x + k) % NX for k in (2, 1, 3)]
    along_z = [at(z=p) for p in z_peers]
    along_y = [at(y=p) for p in y_peers]
    along_x = [at(col=col - x + p) for p in x_peers]
    other = at(core=1 - core)
    far = at(col=(col + NX) % (2 * NX))

    def copy(src, dst, sems, send_at, recv_at, to):
        return pltpu.make_async_remote_copy(
            src_ref=src, dst_ref=dst, send_sem=sems.at[(0, *send_at)], recv_sem=sems.at[(1, *recv_at)],
            device_id=to, device_id_type=MESH,
        )

    started = []

    def send(*args):
        c = copy(*args)
        c.start()
        started.append(c)

    def arrive(dst, sems, recv_at):
        copy(dst, dst, sems, recv_at, recv_at, other).wait_recv()

    loads = [
        pltpu.make_async_copy(ref, weights.at[i], w_sem.at[i]) for i, ref in enumerate((w_up_ref, w_down_ref))
    ]
    for c in loads:
        c.start()

    barrier = pltpu.get_barrier_semaphore()
    everyone = [*along_z, *along_y, *along_x, other, far]
    for d in everyone:
        pl.semaphore_signal(barrier, inc=1, device_id=d, device_id_type=MESH)

    for s, ref in enumerate((tok_ref, grad_ref)):
        v = ref[...].astype(F32)
        folded = jnp.concatenate([v[:, 384 * c : 384 * (c + 1)] for c in range(4)], axis=0)
        pieces[s, y, core, z] = folded.astype(BF16)
    pl.semaphore_wait(barrier, len(everyone))

    for s in range(2):
        mine = pieces.at[s, y, core, z]
        for p, d in zip(z_peers, along_z, strict=True):
            send(mine, mine, az, (s, p), (s, z), d)
    for s in range(2):
        for p in reversed(z_peers):
            arrive(pieces.at[s, y, core, p], az, (s, p))
        mine = pieces.at[s, y, core]
        for p, d in zip(y_peers, along_y, strict=True):
            send(mine, mine, ay, (s, p), (s, y), d)
        send(mine, mine, ac, (s, y), (s, y), other)

    top = lax.broadcasted_iota(jnp.int32, (NZ, 8, 384), 1) < 4

    def gather_rest(s):
        for p in (y_peers[1], y_peers[2], y_peers[0]):
            block = pieces.at[s, p, core]
            arrive(block, ay, (s, p))
            send(block, block, ac, (s, p), (s, p), other)
        for q in range(NY):
            arrive(pieces.at[s, q, 1 - core], ac, (s, q))
        for q in range(NY):
            halves = [pieces[s, q, k].astype(F32).reshape(NZ, 2, 8, 384) for k in range(2)]
            for c in range(4):
                first, second = halves[0][:, c // 2], halves[1][:, c // 2]
                if c % 2 == 0:
                    block = jnp.where(top, first, pltpu.roll(second, 4, 1))
                else:
                    block = jnp.where(top, pltpu.roll(first, 4, 1), second)
                full[s, 64 * q : 64 * (q + 1), 384 * c : 384 * (c + 1)] = block.reshape(64, 384).astype(BF16)

    for s in range(2):
        gather_rest(s)
        loads[s].wait()
        for q in range(NX):
            part[s, q] = along_rows(full[s, 64 * q : 64 * (q + 1), :], weights[s]).astype(BF16)
        for p, d in zip(x_peers, along_x, strict=True):
            send(part.at[s, p], xin.at[s, x], xr, (s, p), (s, x), d)
    for s in range(2):
        total = part[s, x].astype(F32)
        for p in (x_peers[1], x_peers[2], x_peers[0]):
            arrive(xin.at[s, p], xr, (s, p))
            total += xin[s, p].astype(F32)
        far_out[s] = total.astype(BF16)
        send(far_out.at[s], far_in.at[s], fz, (s,), (s,), far)
    sums = []
    for s in range(2):
        arrive(far_in.at[s], fz, (s,))
        sums.append(far_out[s].astype(F32) + far_in[s].astype(F32))
        if s == 0:
            hidden[0, x] = gelu_value(sums[0]).astype(BF16)
        else:
            hidden[1, x] = (sums[1] * gelu_slope(sums[0])).astype(BF16)
        mine = hidden.at[s, x]
        for p, d in zip(x_peers, along_x, strict=True):
            send(mine, mine, xa, (s, p), (s, x), d)

    own = pl.multiple_of(core * 768, 128)
    not_own = pl.multiple_of((1 - core) * 768, 128)
    for s in range(2):
        for p in (x_peers[1], x_peers[2], x_peers[0]):
            arrive(hidden.at[s, p], xa, (s, p))
        w = weights.at[1 - s]
        h = hidden[s].reshape(256, 384)
        core_out[s] = jnp.dot(h, w[:, pl.ds(not_own, 768)], preferred_element_type=F32).astype(BF16)
        send(core_out.at[s], core_in.at[s], rc, (s,), (s,), other)
    for s in range(2):
        h = hidden[s].reshape(256, 384)
        part_out = jnp.dot(h, weights[1 - s, :, pl.ds(own, 768)], preferred_element_type=F32)
        arrive(core_in.at[s], rc, (s,))
        y_out[s] = (part_out + core_in[s].astype(F32)).astype(BF16).reshape(NY, 64, 768)
        for p, d in zip(y_peers, along_y, strict=True):
            send(y_out.at[s, p], y_in.at[s, y], ry, (s, p), (s, y), d)

    stores = []
    for s, ref in ((1, gwd_ref), (0, gwu_ref)):
        h = hidden[1 - s].reshape(256, 384)
        for c in range(4):
            cols = slice(384 * c, 384 * (c + 1))
            wouts[s, :, cols] = (over_tokens(h, full[s, :, cols]) * scale).astype(BF16)
        c = pltpu.make_async_copy(wouts.at[s], ref, o_sem.at[s])
        c.start()
        stores.append(c)

    for s in range(2):
        total = y_out[s, y].astype(F32)
        for p in (y_peers[1], y_peers[2], y_peers[0]):
            arrive(y_in.at[s, p], ry, (s, p))
            total += y_in[s, p].astype(F32)
        rows = total.reshape(NZ, 8, 768)
        z_out[s] = jnp.concatenate([rows[:, :, :384], rows[:, :, 384:]], axis=1).astype(BF16)
        for p, d in zip(z_peers, along_z, strict=True):
            send(z_out.at[s, p], z_in.at[s, z], rz, (s, p), (s, z), d)
    for s in range(2):
        total = z_out[s, z].astype(F32)
        for p in reversed(z_peers):
            arrive(z_in.at[s, p], rz, (s, p))
            total += z_in[s, p].astype(F32)
        last_out[s] = total.astype(BF16)
        send(last_out.at[s], last_in.at[s], rl, (s,), (s,), other)
    for s, ref in ((0, out_ref), (1, gin_ref)):
        arrive(last_in.at[s], rl, (s,))
        mine, theirs = last_out[s].astype(F32), last_in[s].astype(F32)
        left = jnp.where(core == 0, mine, theirs)
        right = jnp.where(core == 0, theirs, mine)
        rows = jnp.concatenate([left[:8], left[8:], right[:8], right[8:]], axis=1)
        ref[...] = jnp.where(core == 0, rows[:4], rows[4:]).astype(BF16)
    for c in started:
        c.wait_send()
    for c in stores:
        c.wait()


def local(tokens, w_up, w_down, grad_out):
    n_tokens = tokens.shape[0] * lax.axis_size("depth") * lax.axis_size("row")
    scale = 1.0 / math.sqrt(n_tokens)
    vmem, hbm = pl.BlockSpec(memory_space=pltpu.VMEM), pl.BlockSpec(memory_space=pl.ANY)
    dma = pltpu.SemaphoreType.DMA
    shape = jax.ShapeDtypeStruct
    return pl.pallas_call(
        functools.partial(kernel, scale),
        name="ffn",
        out_shape=(
            shape((4, 1536), BF16), shape((4, 1536), BF16), shape((384, 1536), BF16), shape((384, 1536), BF16),
        ),
        in_specs=[vmem, hbm, hbm, vmem],
        out_specs=(vmem, vmem, hbm, hbm),
        scratch_shapes=[
            pltpu.VMEM((2, 384, 1536), BF16),
            pltpu.VMEM((2, 384, 1536), BF16),
            pltpu.VMEM((2, NY, 2, NZ, 16, 384), BF16),
            pltpu.VMEM((2, 256, 1536), BF16),
            pltpu.VMEM((2, NX, 64, 384), BF16),
            pltpu.VMEM((2, NX, 64, 384), BF16),
            pltpu.VMEM((2, 64, 384), BF16),
            pltpu.VMEM((2, 64, 384), BF16),
            pltpu.VMEM((2, NX, 64, 384), BF16),
            pltpu.VMEM((2, 256, 768), BF16),
            pltpu.VMEM((2, 256, 768), BF16),
            pltpu.VMEM((2, NY, 64, 768), BF16),
            pltpu.VMEM((2, NY, 64, 768), BF16),
            pltpu.VMEM((2, NZ, 16, 384), BF16),
            pltpu.VMEM((2, NZ, 16, 384), BF16),
            pltpu.VMEM((2, 16, 384), BF16),
            pltpu.VMEM((2, 16, 384), BF16),
            dma((2,)), dma((2,)),
            dma((2, 2, NZ)), dma((2, 2, NY)), dma((2, 2, NY)), dma((2, 2, NX)), dma((2, 2)), dma((2, 2, NX)),
            dma((2, 2)), dma((2, 2, NY)), dma((2, 2, NZ)), dma((2, 2)),
        ],
        compiler_params=pltpu.CompilerParams(
            collective_id=0, has_side_effects=True, vmem_limit_bytes=48 << 20
        ),
    )(tokens, w_up, w_down, grad_out)


def solution(mesh):
    spec = P(("depth", "row"), "col")
    return jax.shard_map(
        local, mesh=mesh, in_specs=(spec,) * 4, out_specs=(spec,) * 4, check_vma=False
    )
```

```python
import functools
import math

import jax
import jax.numpy as jnp
from jax import lax
from jax.experimental import pallas as pl
from jax.experimental.pallas import tpu as pltpu
from jax.sharding import PartitionSpec as P

MESH = pl.DeviceIdType.MESH
NX, NY, NZ = 4, 4, 8
F32, BF16 = jnp.float32, jnp.bfloat16
coeff = 0.7978845608028654


def gelu_value(value):
    inner = jnp.tanh(coeff * (value + 0.044715 * value * value * value))
    return 0.5 * value * (1.0 + inner)


def gelu_slope(value):
    inner = jnp.tanh(coeff * (value + 0.044715 * value * value * value))
    return 0.5 * (1.0 + inner) + 0.5 * value * (1.0 - inner * inner) * coeff * (
        1.0 + 3.0 * 0.044715 * value * value
    )


def along_rows(left, right):
    return lax.dot_general(left, right, (((1,), (1,)), ((), ())), preferred_element_type=F32)


def over_tokens(left, right):
    return lax.dot_general(left, right, (((0,), (0,)), ((), ())), preferred_element_type=F32)


def kernel(
    scale,
    tok_ref, w_up_ref, w_down_ref, grad_ref,
    out_ref, gin_ref, gwu_ref, gwd_ref,
    rows_in, weights, pieces, full, part, xin, far_out, far_in, hidden,
    core_out, core_in, y_out, y_in, z_out, z_in, last_out, last_in,
    r_sem, w_sem, az, ay, ac, xr, fz, xa, rc, ry, rz, rl,
):
    depth, row, col = lax.axis_index("depth"), lax.axis_index("row"), lax.axis_index("col")
    z, y, core, x = depth, row // 2, row % 2, col % NX

    def at(z=depth, y=y, core=core, col=col):
        return {"depth": z, "row": y * 2 + core, "col": col}

    half = z // 4
    near_z = [4 * half + (z + k) % 4 for k in (2, 1, 3)]
    far_z = [4 * (1 - half) + (z + k) % 4 for k in range(4)]
    z_peers = [*far_z, *near_z]
    y_peers = [(y + k) % NY for k in (2, 1, 3)]
    x_peers = [(x + k) % NX for k in (2, 1, 3)]
    y_order = (y_peers[1], y_peers[2], y_peers[0])
    x_order = (x_peers[1], x_peers[2], x_peers[0])
    along_z = [at(z=p) for p in z_peers]
    along_y = [at(y=p) for p in y_peers]
    along_x = [at(col=col - x + p) for p in x_peers]
    other = at(core=1 - core)
    far = at(col=(col + NX) % (2 * NX))

    barrier = pltpu.get_barrier_semaphore()
    everyone = [far, *along_z, *along_y, *along_x, other]
    for d in everyone:
        pl.semaphore_signal(barrier, inc=1, device_id=d, device_id_type=MESH)
    row_loads = [pltpu.make_async_copy(ref, rows_in.at[i], r_sem.at[i]) for i, ref in enumerate((tok_ref, grad_ref))]
    loads = [pltpu.make_async_copy(ref, weights.at[i], w_sem.at[i]) for i, ref in enumerate((w_up_ref, w_down_ref))]
    for c in (*row_loads, *loads):
        c.start()

    def copy(src, dst, sems, send_at, recv_at, to):
        return pltpu.make_async_remote_copy(
            src_ref=src, dst_ref=dst, send_sem=sems.at[(0, *send_at)], recv_sem=sems.at[(1, *recv_at)],
            device_id=to, device_id_type=MESH,
        )

    started = []

    def send(*args):
        c = copy(*args)
        c.start()
        started.append(c)

    def arrive(dst, sems, recv_at):
        copy(dst, dst, sems, recv_at, recv_at, other).wait_recv()

    for s in range(2):
        row_loads[s].wait()
        v = rows_in[s].astype(F32)
        folded = jnp.concatenate([v[:, 384 * c : 384 * (c + 1)] for c in range(4)], axis=0)
        pieces[s, y, core, z] = folded.astype(BF16)
    pl.semaphore_wait(barrier, len(everyone))

    for s in range(2):
        mine = pieces.at[s, y, core, z]
        for p, d in zip(z_peers, along_z, strict=True):
            send(mine, mine, az, (s, p), (s, z), d)

    def part_of(s, q, k, h):
        return pieces.at[s, q, k, pl.ds(4 * (half if h == 0 else 1 - half), 4)]

    def over_y(s, h):
        for p in near_z if h == 0 else reversed(far_z):
            arrive(pieces.at[s, y, core, p], az, (s, p))
        mine = part_of(s, y, core, h)
        for p, d in zip(y_peers, along_y, strict=True):
            send(mine, mine, ay, (s, h, p), (s, h, y), d)
        send(mine, mine, ac, (s, h, y), (s, h, y), other)

    def pass_on(s, h):
        for p in y_order:
            block = part_of(s, p, core, h)
            arrive(block, ay, (s, h, p))
            send(block, block, ac, (s, h, p), (s, h, p), other)

    top = lax.broadcasted_iota(jnp.int32, (NZ, 8, 384), 1) < 4

    def block_of(s, q):
        for h in range(2):
            arrive(part_of(s, q, 1 - core, h), ac, (s, h, q))
        halves = [pieces[s, q, k].astype(F32).reshape(NZ, 2, 8, 384) for k in range(2)]
        rows = pl.ds(pl.multiple_of(64 * q, 64), 64)
        for c in range(4):
            first, second = halves[0][:, c // 2], halves[1][:, c // 2]
            if c % 2 == 0:
                block = jnp.where(top, first, pltpu.roll(second, 4, 1))
            else:
                block = jnp.where(top, pltpu.roll(first, 4, 1), second)
            full[s, rows, 384 * c : 384 * (c + 1)] = block.reshape(64, 384).astype(BF16)
        part[s, q] = along_rows(full[s, rows, :], weights[s]).astype(BF16)

        @pl.when(q != x)
        def _():
            copy(part.at[s, q], xin.at[s, x], xr, (s, q), (s, x), at(col=col - x + q)).start()

    over_y(0, 0)
    over_y(0, 1)
    over_y(1, 0)
    pass_on(0, 0)
    over_y(1, 1)
    loads[0].wait()
    block_of(0, y)
    pass_on(0, 1)
    for p in y_order:
        block_of(0, p)
    pass_on(1, 0)
    loads[1].wait()
    block_of(1, y)
    pass_on(1, 1)
    for p in y_order:
        block_of(1, p)

    for s in range(2):
        total = part[s, x].astype(F32)
        for p in x_order:
            arrive(xin.at[s, p], xr, (s, p))
            total += xin[s, p].astype(F32)
        far_out[s] = total.astype(BF16)
        send(far_out.at[s], far_in.at[s], fz, (s,), (s,), far)

    own = pl.multiple_of(core * 768, 128)
    not_own = pl.multiple_of((1 - core) * 768, 128)

    def summed(s):
        arrive(far_in.at[s], fz, (s,))
        return far_out[s].astype(F32) + far_in[s].astype(F32)

    def over_x(s, value):
        hidden[s, x] = value.astype(BF16)
        mine = hidden.at[s, x]
        for p, d in zip(x_peers, along_x, strict=True):
            send(mine, mine, xa, (s, p), (s, x), d)

    def to_core(s):
        for p in x_order:
            arrive(hidden.at[s, p], xa, (s, p))
        h = hidden[s].reshape(256, 384)
        core_out[s] = jnp.dot(h, weights[1 - s, :, pl.ds(not_own, 768)], preferred_element_type=F32).astype(BF16)
        send(core_out.at[s], core_in.at[s], rc, (s,), (s,), other)

    def to_y(s):
        h = hidden[s].reshape(256, 384)
        part_out = jnp.dot(h, weights[1 - s, :, pl.ds(own, 768)], preferred_element_type=F32)
        arrive(core_in.at[s], rc, (s,))
        y_out[s] = (part_out + core_in[s].astype(F32)).astype(BF16).reshape(NY, 64, 768)
        for p, d in zip(y_peers, along_y, strict=True):
            send(y_out.at[s, p], y_in.at[s, y], ry, (s, p), (s, y), d)

    def weight_grad(s, ref):
        h = hidden[1 - s].reshape(256, 384)
        for c in range(4):
            cols = slice(384 * c, 384 * (c + 1))
            ref[:, cols] = (over_tokens(h, full[s, :, cols]) * scale).astype(BF16)

    def to_z(s):
        total = y_out[s, y].astype(F32)
        for p in y_order:
            arrive(y_in.at[s, p], ry, (s, p))
            total += y_in[s, p].astype(F32)
        rows = total.reshape(NZ, 8, 768)
        z_out[s] = jnp.concatenate([rows[:, :, :384], rows[:, :, 384:]], axis=1).astype(BF16)
        for p, d in zip(z_peers, along_z, strict=True):
            send(z_out.at[s, p], z_in.at[s, z], rz, (s, p), (s, z), d)

    def to_last(s):
        total = z_out[s, z].astype(F32)
        for p in (*near_z, *far_z):
            arrive(z_in.at[s, p], rz, (s, p))
            total += z_in[s, p].astype(F32)
        last_out[s] = total.astype(BF16)
        send(last_out.at[s], last_in.at[s], rl, (s,), (s,), other)

    def finish(s, ref):
        arrive(last_in.at[s], rl, (s,))
        mine, theirs = last_out[s].astype(F32), last_in[s].astype(F32)
        left = jnp.where(core == 0, mine, theirs)
        right = jnp.where(core == 0, theirs, mine)
        rows = jnp.concatenate([left[:8], left[8:], right[:8], right[8:]], axis=1)
        ref[...] = jnp.where(core == 0, rows[:4], rows[4:]).astype(BF16)

    pre = summed(0)
    over_x(0, gelu_value(pre))
    slope = gelu_slope(pre)
    to_core(0)
    over_x(1, summed(1) * slope)
    to_y(0)
    to_core(1)
    to_y(1)
    weight_grad(1, gwd_ref)
    to_z(0)
    weight_grad(0, gwu_ref)
    to_z(1)
    to_last(0)
    finish(0, out_ref)
    to_last(1)
    finish(1, gin_ref)
    for c in started:
        c.wait_send()
    for s in range(2):
        for p in x_peers:
            copy(part.at[s, p], xin.at[s, x], xr, (s, p), (s, x), other).wait_send()


def write_out(*refs):
    sources, targets, sem = refs[:4], refs[4:8], refs[8]
    copies = [pltpu.make_async_copy(a, b, sem.at[i]) for i, (a, b) in enumerate(zip(sources, targets, strict=True))]
    for c in copies:
        c.start()
    for c in copies:
        c.wait()


def local(tokens, w_up, w_down, grad_out):
    n_tokens = tokens.shape[0] * lax.axis_size("depth") * lax.axis_size("row")
    scale = 1.0 / math.sqrt(n_tokens)
    vmem, hbm = pl.BlockSpec(memory_space=pltpu.VMEM), pl.BlockSpec(memory_space=pltpu.HBM)
    dma = pltpu.SemaphoreType.DMA
    shape = jax.ShapeDtypeStruct
    shapes = (
        shape((4, 1536), BF16), shape((4, 1536), BF16), shape((384, 1536), BF16), shape((384, 1536), BF16),
    )
    held = pltpu.with_memory_space_constraint
    results = pl.pallas_call(
        functools.partial(kernel, scale),
        name="ffn",
        out_shape=tuple(pltpu.VMEM(a.shape, a.dtype) for a in shapes),
        in_specs=[hbm] * 4,
        out_specs=(vmem,) * 4,
        scratch_shapes=[
            pltpu.VMEM((2, 4, 1536), BF16),
            pltpu.VMEM((2, 384, 1536), BF16),
            pltpu.VMEM((2, NY, 2, NZ, 16, 384), BF16),
            pltpu.VMEM((2, 256, 1536), BF16),
            pltpu.VMEM((2, NX, 64, 384), BF16),
            pltpu.VMEM((2, NX, 64, 384), BF16),
            pltpu.VMEM((2, 64, 384), BF16),
            pltpu.VMEM((2, 64, 384), BF16),
            pltpu.VMEM((2, NX, 64, 384), BF16),
            pltpu.VMEM((2, 256, 768), BF16),
            pltpu.VMEM((2, 256, 768), BF16),
            pltpu.VMEM((2, NY, 64, 768), BF16),
            pltpu.VMEM((2, NY, 64, 768), BF16),
            pltpu.VMEM((2, NZ, 16, 384), BF16),
            pltpu.VMEM((2, NZ, 16, 384), BF16),
            pltpu.VMEM((2, 16, 384), BF16),
            pltpu.VMEM((2, 16, 384), BF16),
            dma((2,)), dma((2,)),
            dma((2, 2, NZ)), dma((2, 2, 2, NY)), dma((2, 2, 2, NY)), dma((2, 2, NX)), dma((2, 2)), dma((2, 2, NX)),
            dma((2, 2)), dma((2, 2, NY)), dma((2, 2, NZ)), dma((2, 2)),
        ],
        compiler_params=pltpu.CompilerParams(
            collective_id=0, has_side_effects=True, vmem_limit_bytes=48 << 20
        ),
    )(*(held(a, pltpu.HBM) for a in (tokens, w_up, w_down, grad_out)))
    return pl.pallas_call(
        write_out,
        name="write_out",
        out_shape=tuple(pltpu.HBM(a.shape, a.dtype) for a in shapes),
        in_specs=[vmem] * 4,
        out_specs=(hbm,) * 4,
        scratch_shapes=[dma((4,))],
    )(*(held(a, pltpu.VMEM) for a in results))


def solution(mesh):
    spec = P(("depth", "row"), "col")
    return jax.shard_map(
        local, mesh=mesh, in_specs=(spec,) * 4, out_specs=(spec,) * 4, check_vma=False
    )
```

```python
import functools
import math

import jax
import jax.numpy as jnp
from jax import lax
from jax.experimental import pallas as pl
from jax.experimental.pallas import tpu as pltpu
from jax.sharding import PartitionSpec as P

MESH = pl.DeviceIdType.MESH
NX, NY, NZ = 4, 4, 8
F32, BF16 = jnp.float32, jnp.bfloat16
coeff = 0.7978845608028654


def gelu_value(value):
    inner = jnp.tanh(coeff * (value + 0.044715 * value * value * value))
    return 0.5 * value * (1.0 + inner)


def gelu_slope(value):
    inner = jnp.tanh(coeff * (value + 0.044715 * value * value * value))
    return 0.5 * (1.0 + inner) + 0.5 * value * (1.0 - inner * inner) * coeff * (
        1.0 + 3.0 * 0.044715 * value * value
    )


def along_rows(left, right):
    return lax.dot_general(left, right, (((1,), (1,)), ((), ())), preferred_element_type=F32)


def over_tokens(left, right):
    return lax.dot_general(left, right, (((0,), (0,)), ((), ())), preferred_element_type=F32)


def kernel(
    scale,
    tok_ref, w_up_ref, w_down_ref, grad_ref,
    out_ref, gin_ref, gwu_ref, gwd_ref,
    rows_in, weights, lent, pieces, full, part, xin, far_out, far_in, slopes_out, slopes, hidden,
    y_out, y_in, z_out, z_in, last_out, last_in,
    r_sem, w_sem, wx, cx, az, ay, fx, xr, fz, sx, xa, hx, ry, rz, lx,
):
    depth, row, col = lax.axis_index("depth"), lax.axis_index("row"), lax.axis_index("col")
    z, y, core, x = depth, row // 2, row % 2, col % NX

    def at(z=depth, y=y, core=core, col=col):
        return {"depth": z, "row": y * 2 + core, "col": col}

    half = z // 4
    near_z = [4 * half + (z + k) % 4 for k in (2, 1, 3)]
    far_z = [4 * (1 - half) + (z + k) % 4 for k in range(4)]
    z_peers = [*far_z, *near_z]
    y_peers = [(y + k) % NY for k in (2, 1, 3)]
    x_peers = [(x + k) % NX for k in (2, 1, 3)]
    y_order = (y_peers[1], y_peers[2], y_peers[0])
    x_order = (x_peers[1], x_peers[2], x_peers[0])
    along_z = [at(z=p) for p in z_peers]
    along_y = [at(y=p) for p in y_peers]
    along_x = [at(col=col - x + p) for p in x_peers]
    other = at(core=1 - core)
    far = at(col=(col + NX) % (2 * NX))

    barrier = pltpu.get_barrier_semaphore()
    everyone = [far, *along_z, *along_y, *along_x, other]
    for d in everyone:
        pl.semaphore_signal(barrier, inc=1, device_id=d, device_id_type=MESH)
    row_loads = [pltpu.make_async_copy(ref, rows_in.at[i], r_sem.at[i]) for i, ref in enumerate((tok_ref, grad_ref))]
    loads = [pltpu.make_async_copy(ref, weights.at[i, core], w_sem.at[i]) for i, ref in enumerate((w_up_ref, w_down_ref))]
    for c in (*row_loads, *loads):
        c.start()

    def copy(src, dst, sems, send_at, recv_at, to):
        return pltpu.make_async_remote_copy(
            src_ref=src, dst_ref=dst, send_sem=sems.at[(0, *send_at)], recv_sem=sems.at[(1, *recv_at)],
            device_id=to, device_id_type=MESH,
        )

    started = []

    def send(*args):
        c = copy(*args)
        c.start()
        started.append(c)

    def arrive(dst, sems, recv_at):
        copy(dst, dst, sems, recv_at, recv_at, other).wait_recv()

    for c in row_loads:
        c.wait()

    def folded(s):
        v = rows_in[s].astype(F32)
        return jnp.concatenate([v[:, 384 * c : 384 * (c + 1)] for c in range(4)], axis=0).astype(BF16)

    pieces[core, y, z] = folded(core)
    lent[...] = folded(1 - core)
    pl.semaphore_wait(barrier, len(everyone))

    send(lent, pieces.at[core, y, z], cx, (), (), other)
    for a in range(2):
        mine = pieces.at[a, y, z]

        @pl.when(core != a)
        def _():
            arrive(mine, cx, ())

        for p, d in zip(z_peers, along_z, strict=True):
            send(mine, mine, az, (a, p), (a, z), d)
    for i, ref in enumerate((w_up_ref, w_down_ref)):
        send(ref, weights.at[i, core], wx, (i,), (i,), other)

    def part_of(k, q):
        return pieces.at[k // 2, q, pl.ds(4 * (half if k % 2 == 0 else 1 - half), 4)]

    def over_y(k):
        a = k // 2
        for p in near_z if k % 2 == 0 else reversed(far_z):
            arrive(pieces.at[a, y, p], az, (a, p))
        block = part_of(k, y)
        for p, d in zip(y_peers, along_y, strict=True):
            send(block, block, ay, (k, p), (k, y), d)

    top = lax.broadcasted_iota(jnp.int32, (2, 8, 384), 1) < 4

    def order(k, q):
        v = part_of(k, q)[...].astype(F32).reshape(2, 2, 2, 8, 384)
        rows = pl.ds(pl.multiple_of(16 * q, 16), 16)
        for c in range(4):
            first, second = v[:, 0, c // 2], v[:, 1, c // 2]
            if c % 2 == 0:
                block = jnp.where(top, first, pltpu.roll(second, 4, 1))
            else:
                block = jnp.where(top, pltpu.roll(first, 4, 1), second)
            full[core, k, rows, 384 * c : 384 * (c + 1)] = block.reshape(16, 384).astype(BF16)

    def project(k):
        order(k, y)
        for p in y_order:
            arrive(part_of(k, p), ay, (k, p))
            order(k, p)
        if k == 0:
            for i in range(2):
                loads[i].wait()
                arrive(weights.at[i, 1 - core], wx, (i,))
        for f in range(2):
            part[k, :, f] = along_rows(full[core, k], weights[core, f]).astype(BF16).reshape(NX, 16, 384)
        for p, d in zip(x_peers, along_x, strict=True):
            send(part.at[k, p], xin.at[k, x], xr, (k, p), (k, x), d)
        send(full.at[core, k], full.at[core, k], fx, (k,), (k,), other)

    def to_far(a):
        total = part[a, x].astype(F32)
        for p in x_order:
            arrive(xin.at[a, p], xr, (a, p))
            total += xin[a, p].astype(F32)
        far_out[a] = total.astype(BF16)
        send(far_out.at[a], far_in.at[a], fz, (a,), (a,), far)

    def slope_copy(a):
        return copy(slopes_out.at[a], slopes.at[a], sx, (a,), (a,), other)

    def activate(a):
        arrive(far_in.at[a], fz, (a,))

        @pl.when(core == 0)
        def _():
            pre = far_out[a].astype(F32) + far_in[a].astype(F32)
            slopes_out[a] = gelu_slope(pre)
            slope_copy(a).start()
            hidden[core, a, x] = gelu_value(pre).astype(BF16)

        @pl.when(core == 1)
        def _():
            slope_copy(a).wait_recv()
            grad_act = far_out[a].astype(F32) + far_in[a].astype(F32)
            hidden[core, a, x] = (grad_act * slopes[a]).astype(BF16)

        block = hidden.at[core, a, x]
        for p, d in zip(x_peers, along_x, strict=True):
            send(block, block, xa, (a, p), (a, x), d)

    def back(a):
        for p in x_order:
            arrive(hidden.at[core, a, p], xa, (a, p))
        for n in range(2):
            cols = slice(768 * n, 768 * (n + 1))
            total = sum(
                jnp.dot(
                    hidden[core, a, :, f].reshape(64, 384), weights[1 - core, f, :, cols], preferred_element_type=F32
                )
                for f in range(2)
            )
            y_out[a, :, :, cols] = total.astype(BF16).reshape(NY, 16, 768)
        for p, d in zip(y_peers, along_y, strict=True):
            send(y_out.at[a, p], y_in.at[a, y], ry, (a, p), (a, y), d)
        lend = hidden.at[core, a, :, 1 - core]
        send(lend, lend, hx, (a,), (a,), other)

    def to_z(k):
        total = y_out[k, y].astype(F32)
        for p in y_order:
            arrive(y_in.at[k, p], ry, (k, p))
            total += y_in[k, p].astype(F32)
        rows = total.reshape(2, 8, 1536)
        c = [rows[:, :, 384 * i : 384 * (i + 1)] for i in range(4)]
        for parity in range(2):
            tiles = [
                jnp.where(top, c[2 * r], pltpu.roll(c[2 * r + 1], 4, 1))
                if parity == 0
                else jnp.where(top, pltpu.roll(c[2 * r], 4, 1), c[2 * r + 1])
                for r in range(2)
            ]
            z_out[k, :, parity] = jnp.concatenate(tiles, axis=1).astype(BF16)
        a = k // 2
        for p in near_z if k % 2 == 0 else far_z:
            send(z_out.at[k, p % 4 // 2, p % 2], z_in.at[a, z], rz, (a, p), (a, z), at(z=p))
        if k % 2 == 0:
            z_in[a, z] = z_out[k, z % 4 // 2, z % 2]

    def unfolded(v):
        low, high = v[:8], v[8:]
        return jnp.concatenate([low, pltpu.roll(low, 4, 0), high, pltpu.roll(high, 4, 0)], axis=1)[:4]

    last_copy = copy(last_out, last_in, lx, (), (), other)

    def finish(a, own_ref):
        for p in (*near_z, *far_z):
            arrive(z_in.at[a, p], rz, (a, p))
        total = sum(z_in[a, i].astype(F32) for i in range(NZ))

        @pl.when(core == a)
        def _():
            own_ref[...] = unfolded(total).astype(BF16)

        @pl.when(core != a)
        def _():
            last_out[...] = total.astype(BF16)
            last_copy.start()

    def weight_grad(s, ref):
        h = hidden[1 - s, :, :, core].reshape(256, 384)
        for c in range(4):
            cols = slice(384 * c, 384 * (c + 1))
            ref[:, cols] = (over_tokens(h, full[s, :, :, cols].reshape(256, 384)) * scale).astype(BF16)

    for k in range(4):
        over_y(k)
    project(0)
    project(1)
    to_far(0)
    project(2)
    to_far(1)
    project(3)
    to_far(2)
    to_far(3)
    activate(0)
    activate(1)
    activate(2)
    back(0)
    activate(3)
    back(1)
    back(2)
    to_z(0)
    back(3)
    to_z(1)
    to_z(2)
    to_z(3)
    for k in range(4):
        arrive(full.at[1 - core, k], fx, (k,))
        arrive(hidden.at[1 - core, k, :, core], hx, (k,))
    weight_grad(0, gwu_ref)
    weight_grad(1, gwd_ref)
    finish(0, out_ref)
    finish(1, gin_ref)
    last_copy.wait()
    theirs = unfolded(last_in[...].astype(F32)).astype(BF16)

    @pl.when(core == 0)
    def _():
        gin_ref[...] = theirs
        for k in range(4):
            slope_copy(k).wait_send()

    @pl.when(core == 1)
    def _():
        out_ref[...] = theirs

    for c in started:
        c.wait_send()


def write_out(*refs):
    sources, targets, sem = refs[:4], refs[4:8], refs[8]
    copies = [pltpu.make_async_copy(a, b, sem.at[i]) for i, (a, b) in enumerate(zip(sources, targets, strict=True))]
    for c in copies:
        c.start()
    for c in copies:
        c.wait()


def local(tokens, w_up, w_down, grad_out):
    n_tokens = tokens.shape[0] * lax.axis_size("depth") * lax.axis_size("row")
    scale = 1.0 / math.sqrt(n_tokens)
    vmem, hbm = pl.BlockSpec(memory_space=pltpu.VMEM), pl.BlockSpec(memory_space=pltpu.HBM)
    dma = pltpu.SemaphoreType.DMA
    shape = jax.ShapeDtypeStruct
    shapes = (
        shape((4, 1536), BF16), shape((4, 1536), BF16), shape((384, 1536), BF16), shape((384, 1536), BF16),
    )
    held = pltpu.with_memory_space_constraint
    results = pl.pallas_call(
        functools.partial(kernel, scale),
        name="ffn",
        out_shape=tuple(pltpu.VMEM(a.shape, a.dtype) for a in shapes),
        in_specs=[hbm] * 4,
        out_specs=(vmem,) * 4,
        scratch_shapes=[
            pltpu.VMEM((2, 4, 1536), BF16),
            pltpu.VMEM((2, 2, 384, 1536), BF16),
            pltpu.VMEM((16, 384), BF16),
            pltpu.VMEM((2, NY, NZ, 16, 384), BF16),
            pltpu.VMEM((2, 4, 64, 1536), BF16),
            pltpu.VMEM((4, NX, 2, 16, 384), BF16),
            pltpu.VMEM((4, NX, 2, 16, 384), BF16),
            pltpu.VMEM((4, 2, 16, 384), BF16),
            pltpu.VMEM((4, 2, 16, 384), BF16),
            pltpu.VMEM((4, 2, 16, 384), F32),
            pltpu.VMEM((4, 2, 16, 384), F32),
            pltpu.VMEM((2, 4, NX, 2, 16, 384), BF16),
            pltpu.VMEM((4, NY, 16, 1536), BF16),
            pltpu.VMEM((4, NY, 16, 1536), BF16),
            pltpu.VMEM((4, 2, 2, 16, 384), BF16),
            pltpu.VMEM((2, NZ, 16, 384), BF16),
            pltpu.VMEM((16, 384), BF16),
            pltpu.VMEM((16, 384), BF16),
            dma((2,)), dma((2,)), dma((2, 2)), dma((2,)),
            dma((2, 2, NZ)), dma((2, 4, NY)), dma((2, 4)), dma((2, 4, NX)), dma((2, 4)), dma((2, 4)), dma((2, 4, NX)),
            dma((2, 4)), dma((2, 4, NY)), dma((2, 2, NZ)), dma((2,)),
        ],
        compiler_params=pltpu.CompilerParams(
            collective_id=0, has_side_effects=True, vmem_limit_bytes=48 << 20
        ),
    )(*(held(a, pltpu.HBM) for a in (tokens, w_up, w_down, grad_out)))
    return pl.pallas_call(
        write_out,
        name="write_out",
        out_shape=tuple(pltpu.HBM(a.shape, a.dtype) for a in shapes),
        in_specs=[vmem] * 4,
        out_specs=(hbm,) * 4,
        scratch_shapes=[dma((4,))],
    )(*(held(a, pltpu.VMEM) for a in results))


def solution(mesh):
    spec = P(("depth", "row"), "col")
    return jax.shard_map(
        local, mesh=mesh, in_specs=(spec,) * 4, out_specs=(spec,) * 4, check_vma=False
    )
```

```python
import functools
import math

import jax
import jax.numpy as jnp
from jax import lax
from jax.experimental import pallas as pl
from jax.experimental.pallas import tpu as pltpu
from jax.sharding import PartitionSpec as P

MESH = pl.DeviceIdType.MESH
NX, NY, NZ = 4, 4, 8
F32, BF16 = jnp.float32, jnp.bfloat16
coeff = 0.7978845608028654


def gelu_value(value):
    inner = jnp.tanh(coeff * (value + 0.044715 * value * value * value))
    return 0.5 * value * (1.0 + inner)


def gelu_slope(value):
    inner = jnp.tanh(coeff * (value + 0.044715 * value * value * value))
    return 0.5 * (1.0 + inner) + 0.5 * value * (1.0 - inner * inner) * coeff * (
        1.0 + 3.0 * 0.044715 * value * value
    )


def along_rows(left, right):
    return lax.dot_general(left, right, (((1,), (1,)), ((), ())), preferred_element_type=F32)


def over_tokens(left, right):
    return lax.dot_general(left, right, (((0,), (0,)), ((), ())), preferred_element_type=F32)


def kernel(
    scale,
    tok_ref, w_up_ref, w_down_ref, grad_ref,
    out_ref, gin_ref, gwu_ref, gwd_ref,
    rows_in, weights, lent, pieces, full, part, xin, far_out, far_in, slopes_out, slopes, hidden,
    y_out, y_in, z_out, z_in, jump_out, jump_in, last_out, last_in,
    r_sem, w_sem, wx, cx, az, ay, fx, xr, fz, sx, xa, hx, ry, rz, rj, lx,
):
    depth, row, col = lax.axis_index("depth"), lax.axis_index("row"), lax.axis_index("col")
    z, y, core, x = depth, row // 2, row % 2, col % NX

    def at(z=depth, y=y, core=core, col=col):
        return {"depth": z, "row": y * 2 + core, "col": col}

    half = z // 4
    near_z = [4 * half + (z + k) % 4 for k in (2, 1, 3)]
    jump = 4 * (1 - half) + z % 4
    y_peers = [(y + k) % NY for k in (2, 1, 3)]
    x_peers = [(x + k) % NX for k in (2, 1, 3)]
    y_order = (y_peers[1], y_peers[2], y_peers[0])
    x_order = (x_peers[1], x_peers[2], x_peers[0])
    along_z = [at(z=p) for p in near_z]
    over = at(z=jump)
    along_y = [at(y=p) for p in y_peers]
    along_x = [at(col=col - x + p) for p in x_peers]
    other = at(core=1 - core)
    far = at(col=(col + NX) % (2 * NX))

    barrier = pltpu.get_barrier_semaphore()
    everyone = [far, over, *along_z, *along_y, *along_x, other]
    for d in everyone:
        pl.semaphore_signal(barrier, inc=1, device_id=d, device_id_type=MESH)
    row_loads = [pltpu.make_async_copy(ref, rows_in.at[i], r_sem.at[i]) for i, ref in enumerate((tok_ref, grad_ref))]
    loads = [pltpu.make_async_copy(ref, weights.at[i, core], w_sem.at[i]) for i, ref in enumerate((w_up_ref, w_down_ref))]
    for c in (*row_loads, *loads):
        c.start()

    def copy(src, dst, sems, send_at, recv_at, to):
        return pltpu.make_async_remote_copy(
            src_ref=src, dst_ref=dst, send_sem=sems.at[(0, *send_at)], recv_sem=sems.at[(1, *recv_at)],
            device_id=to, device_id_type=MESH,
        )

    started = []

    def send(*args):
        c = copy(*args)
        c.start()
        started.append(c)

    def arrive(dst, sems, recv_at):
        copy(dst, dst, sems, recv_at, recv_at, other).wait_recv()

    for c in row_loads:
        c.wait()

    def folded(s):
        v = rows_in[s].astype(F32)
        return jnp.concatenate([v[:, 384 * c : 384 * (c + 1)] for c in range(4)], axis=0).astype(BF16)

    pieces[core, y, z] = folded(core)
    lent[...] = folded(1 - core)
    pl.semaphore_wait(barrier, len(everyone))

    send(lent, pieces.at[core, y, z], cx, (), (), other)
    for a in range(2):
        mine = pieces.at[a, y, z]

        @pl.when(core != a)
        def _():
            arrive(mine, cx, ())

        send(mine, mine, az, (a, jump), (a, z), over)
        for p, d in zip(near_z, along_z, strict=True):
            send(mine, mine, az, (a, p), (a, z), d)
    for i, ref in enumerate((w_up_ref, w_down_ref)):
        send(ref, weights.at[i, core], wx, (i,), (i,), other)

    def crossed(p):
        return 4 * (1 - half) + p % 4

    def pass_on(a):
        block = pieces.at[a, y, jump]
        arrive(block, az, (a, jump))
        for p, d in zip(near_z, along_z, strict=True):
            send(block, block, az, (a, crossed(p)), (a, jump), d)

    def part_of(k, q):
        return pieces.at[k // 2, q, pl.ds(4 * (half if k % 2 == 0 else 1 - half), 4)]

    def over_y(k):
        a = k // 2
        for p in near_z:
            p = p if k % 2 == 0 else crossed(p)
            arrive(pieces.at[a, y, p], az, (a, p))
        block = part_of(k, y)
        for p, d in zip(y_peers, along_y, strict=True):
            send(block, block, ay, (k, p), (k, y), d)

    top = lax.broadcasted_iota(jnp.int32, (2, 8, 384), 1) < 4

    def order(k, q):
        v = part_of(k, q)[...].astype(F32).reshape(2, 2, 2, 8, 384)
        rows = pl.ds(pl.multiple_of(16 * q, 16), 16)
        for c in range(4):
            first, second = v[:, 0, c // 2], v[:, 1, c // 2]
            if c % 2 == 0:
                block = jnp.where(top, first, pltpu.roll(second, 4, 1))
            else:
                block = jnp.where(top, pltpu.roll(first, 4, 1), second)
            full[core, k, rows, 384 * c : 384 * (c + 1)] = block.reshape(16, 384).astype(BF16)

    def project(k):
        order(k, y)
        for p in y_order:
            arrive(part_of(k, p), ay, (k, p))
            order(k, p)
        if k == 0:
            for i in range(2):
                loads[i].wait()
                arrive(weights.at[i, 1 - core], wx, (i,))
        for f in range(2):
            part[k, :, f] = along_rows(full[core, k], weights[core, f]).astype(BF16).reshape(NX, 16, 384)
        for p, d in zip(x_peers, along_x, strict=True):
            send(part.at[k, p], xin.at[k, x], xr, (k, p), (k, x), d)
        send(full.at[core, k], full.at[core, k], fx, (k,), (k,), other)

    def to_far(a):
        total = part[a, x].astype(F32)
        for p in x_order:
            arrive(xin.at[a, p], xr, (a, p))
            total += xin[a, p].astype(F32)
        far_out[a] = total.astype(BF16)
        send(far_out.at[a], far_in.at[a], fz, (a,), (a,), far)

    def slope_copy(a):
        return copy(slopes_out.at[a], slopes.at[a], sx, (a,), (a,), other)

    def activate(a):
        arrive(far_in.at[a], fz, (a,))

        @pl.when(core == 0)
        def _():
            pre = far_out[a].astype(F32) + far_in[a].astype(F32)
            slopes_out[a] = gelu_slope(pre)
            slope_copy(a).start()
            hidden[core, a, x] = gelu_value(pre).astype(BF16)

        @pl.when(core == 1)
        def _():
            slope_copy(a).wait_recv()
            grad_act = far_out[a].astype(F32) + far_in[a].astype(F32)
            hidden[core, a, x] = (grad_act * slopes[a]).astype(BF16)

        block = hidden.at[core, a, x]
        for p, d in zip(x_peers, along_x, strict=True):
            send(block, block, xa, (a, p), (a, x), d)

    def back(a):
        for p in x_order:
            arrive(hidden.at[core, a, p], xa, (a, p))
        for n in range(2):
            cols = slice(768 * n, 768 * (n + 1))
            total = sum(
                jnp.dot(
                    hidden[core, a, :, f].reshape(64, 384), weights[1 - core, f, :, cols], preferred_element_type=F32
                )
                for f in range(2)
            )
            y_out[a, :, :, cols] = total.astype(BF16).reshape(NY, 16, 768)
        for p, d in zip(y_peers, along_y, strict=True):
            send(y_out.at[a, p], y_in.at[a, y], ry, (a, p), (a, y), d)
        lend = hidden.at[core, a, :, 1 - core]
        send(lend, lend, hx, (a,), (a,), other)

    def to_z(k):
        total = y_out[k, y].astype(F32)
        for p in y_order:
            arrive(y_in.at[k, p], ry, (k, p))
            total += y_in[k, p].astype(F32)
        rows = total.reshape(2, 8, 1536)
        c = [rows[:, :, 384 * i : 384 * (i + 1)] for i in range(4)]
        for parity in range(2):
            tiles = [
                jnp.where(top, c[2 * r], pltpu.roll(c[2 * r + 1], 4, 1))
                if parity == 0
                else jnp.where(top, pltpu.roll(c[2 * r], 4, 1), c[2 * r + 1])
                for r in range(2)
            ]
            z_out[k, :, parity] = jnp.concatenate(tiles, axis=1).astype(BF16)
        mine = z % 4
        for p, d in zip(near_z, along_z, strict=True):
            send(z_out.at[k, p % 4 // 2, p % 2], z_in.at[k, mine], rz, (k, p % 4), (k, mine), d)
        z_in[k, mine] = z_out[k, mine // 2, mine % 2]

    def half_sum(k):
        for p in near_z:
            arrive(z_in.at[k, p % 4], rz, (k, p % 4))
        return sum(z_in[k, i].astype(F32) for i in range(4))

    def cross(a):
        jump_out[a] = half_sum(2 * a + 1).astype(BF16)
        send(jump_out.at[a], jump_in.at[a], rj, (a,), (a,), over)

    def unfolded(v):
        low, high = v[:8], v[8:]
        return jnp.concatenate([low, pltpu.roll(low, 4, 0), high, pltpu.roll(high, 4, 0)], axis=1)[:4]

    last_copy = copy(last_out, last_in, lx, (), (), other)

    def finish(a, own_ref):
        total = half_sum(2 * a)
        arrive(jump_in.at[a], rj, (a,))
        total += jump_in[a].astype(F32)

        @pl.when(core == a)
        def _():
            own_ref[...] = unfolded(total).astype(BF16)

        @pl.when(core != a)
        def _():
            last_out[...] = total.astype(BF16)
            last_copy.start()

    def weight_grad(s, ref):
        h = hidden[1 - s, :, :, core].reshape(256, 384)
        for c in range(4):
            cols = slice(384 * c, 384 * (c + 1))
            ref[:, cols] = (over_tokens(h, full[s, :, :, cols].reshape(256, 384)) * scale).astype(BF16)

    over_y(0)
    pass_on(0)
    over_y(2)
    pass_on(1)
    over_y(1)
    over_y(3)
    project(0)
    project(2)
    to_far(0)
    project(1)
    to_far(2)
    project(3)
    to_far(1)
    to_far(3)
    activate(0)
    activate(2)
    back(0)
    activate(1)
    back(2)
    activate(3)
    back(1)
    to_z(0)
    back(3)
    to_z(2)
    to_z(1)
    for k in range(4):
        arrive(full.at[1 - core, k], fx, (k,))
        arrive(hidden.at[1 - core, k, :, core], hx, (k,))
    weight_grad(0, gwu_ref)
    to_z(3)
    cross(0)
    cross(1)
    weight_grad(1, gwd_ref)
    finish(0, out_ref)
    finish(1, gin_ref)
    last_copy.wait()
    theirs = unfolded(last_in[...].astype(F32)).astype(BF16)

    @pl.when(core == 0)
    def _():
        gin_ref[...] = theirs
        for k in range(4):
            slope_copy(k).wait_send()

    @pl.when(core == 1)
    def _():
        out_ref[...] = theirs

    for c in started:
        c.wait_send()


def write_out(*refs):
    sources, targets, sem = refs[:4], refs[4:8], refs[8]
    copies = [pltpu.make_async_copy(a, b, sem.at[i]) for i, (a, b) in enumerate(zip(sources, targets, strict=True))]
    for c in copies:
        c.start()
    for c in copies:
        c.wait()


def local(tokens, w_up, w_down, grad_out):
    n_tokens = tokens.shape[0] * lax.axis_size("depth") * lax.axis_size("row")
    scale = 1.0 / math.sqrt(n_tokens)
    vmem, hbm = pl.BlockSpec(memory_space=pltpu.VMEM), pl.BlockSpec(memory_space=pltpu.HBM)
    dma = pltpu.SemaphoreType.DMA
    shape = jax.ShapeDtypeStruct
    shapes = (
        shape((4, 1536), BF16), shape((4, 1536), BF16), shape((384, 1536), BF16), shape((384, 1536), BF16),
    )
    held = pltpu.with_memory_space_constraint
    results = pl.pallas_call(
        functools.partial(kernel, scale),
        name="ffn",
        out_shape=tuple(pltpu.VMEM(a.shape, a.dtype) for a in shapes),
        in_specs=[hbm] * 4,
        out_specs=(vmem,) * 4,
        scratch_shapes=[
            pltpu.VMEM((2, 4, 1536), BF16),
            pltpu.VMEM((2, 2, 384, 1536), BF16),
            pltpu.VMEM((16, 384), BF16),
            pltpu.VMEM((2, NY, NZ, 16, 384), BF16),
            pltpu.VMEM((2, 4, 64, 1536), BF16),
            pltpu.VMEM((4, NX, 2, 16, 384), BF16),
            pltpu.VMEM((4, NX, 2, 16, 384), BF16),
            pltpu.VMEM((4, 2, 16, 384), BF16),
            pltpu.VMEM((4, 2, 16, 384), BF16),
            pltpu.VMEM((4, 2, 16, 384), F32),
            pltpu.VMEM((4, 2, 16, 384), F32),
            pltpu.VMEM((2, 4, NX, 2, 16, 384), BF16),
            pltpu.VMEM((4, NY, 16, 1536), BF16),
            pltpu.VMEM((4, NY, 16, 1536), BF16),
            pltpu.VMEM((4, 2, 2, 16, 384), BF16),
            pltpu.VMEM((4, 4, 16, 384), BF16),
            pltpu.VMEM((2, 16, 384), BF16),
            pltpu.VMEM((2, 16, 384), BF16),
            pltpu.VMEM((16, 384), BF16),
            pltpu.VMEM((16, 384), BF16),
            dma((2,)), dma((2,)), dma((2, 2)), dma((2,)),
            dma((2, 2, NZ)), dma((2, 4, NY)), dma((2, 4)), dma((2, 4, NX)), dma((2, 4)), dma((2, 4)), dma((2, 4, NX)),
            dma((2, 4)), dma((2, 4, NY)), dma((2, 4, 4)), dma((2, 2)), dma((2,)),
        ],
        compiler_params=pltpu.CompilerParams(
            collective_id=0, has_side_effects=True, vmem_limit_bytes=48 << 20
        ),
    )(*(held(a, pltpu.HBM) for a in (tokens, w_up, w_down, grad_out)))
    return pl.pallas_call(
        write_out,
        name="write_out",
        out_shape=tuple(pltpu.HBM(a.shape, a.dtype) for a in shapes),
        in_specs=[vmem] * 4,
        out_specs=(hbm,) * 4,
        scratch_shapes=[dma((4,))],
    )(*(held(a, pltpu.VMEM) for a in results))


def solution(mesh):
    spec = P(("depth", "row"), "col")
    return jax.shard_map(
        local, mesh=mesh, in_specs=(spec,) * 4, out_specs=(spec,) * 4, check_vma=False
    )
```

```python
import functools
import math

import jax
import jax.numpy as jnp
from jax import lax
from jax.experimental import pallas as pl
from jax.experimental.pallas import tpu as pltpu
from jax.sharding import PartitionSpec as P

MESH = pl.DeviceIdType.MESH
NX, NY, NZ = 4, 4, 8
F32, BF16 = jnp.float32, jnp.bfloat16
coeff = 0.7978845608028654


def gelu_value(value):
    inner = jnp.tanh(coeff * (value + 0.044715 * value * value * value))
    return 0.5 * value * (1.0 + inner)


def gelu_slope(value):
    inner = jnp.tanh(coeff * (value + 0.044715 * value * value * value))
    return 0.5 * (1.0 + inner) + 0.5 * value * (1.0 - inner * inner) * coeff * (
        1.0 + 3.0 * 0.044715 * value * value
    )


def along_rows(left, right):
    return lax.dot_general(left, right, (((1,), (1,)), ((), ())), preferred_element_type=F32)


def over_tokens(left, right):
    return lax.dot_general(left, right, (((0,), (0,)), ((), ())), preferred_element_type=F32)


def kernel(
    scale,
    tok_ref, w_up_ref, w_down_ref, grad_ref,
    out_ref, gin_ref, gwu_ref, gwd_ref,
    rows_in, weights, lent, pieces, full, part, xin, far_out, far_in, slopes_out, slopes, hidden,
    y_out, y_in, z_out, z_in, jump_out, jump_in, last_out, last_in,
    r_sem, w_sem, wx, cx, az, ay, fx, xr, fz, sx, xa, hx, ry, rz, rj, lx,
):
    depth, row, col = lax.axis_index("depth"), lax.axis_index("row"), lax.axis_index("col")
    z, y, core, x = depth, row // 2, row % 2, col % NX

    def at(z=depth, y=y, core=core, col=col):
        return {"depth": z, "row": y * 2 + core, "col": col}

    half = z // 4
    near_z = [4 * half + (z + k) % 4 for k in (2, 1, 3)]
    jump = 4 * (1 - half) + z % 4
    y_peers = [(y + k) % NY for k in (2, 1, 3)]
    x_peers = [(x + k) % NX for k in (2, 1, 3)]
    y_order = (y_peers[1], y_peers[2], y_peers[0])
    x_order = (x_peers[1], x_peers[2], x_peers[0])
    along_z = [at(z=p) for p in near_z]
    over = at(z=jump)
    along_y = [at(y=p) for p in y_peers]
    along_x = [at(col=col - x + p) for p in x_peers]
    other = at(core=1 - core)
    far = at(col=(col + NX) % (2 * NX))

    barrier = pltpu.get_barrier_semaphore()
    everyone = [far, over, *along_z, *along_y, *along_x, other]
    for d in everyone:
        pl.semaphore_signal(barrier, inc=1, device_id=d, device_id_type=MESH)
    row_loads = [pltpu.make_async_copy(ref, rows_in.at[i], r_sem.at[i]) for i, ref in enumerate((tok_ref, grad_ref))]
    loads = [pltpu.make_async_copy(ref, weights.at[i, core], w_sem.at[i]) for i, ref in enumerate((w_up_ref, w_down_ref))]
    for c in (*row_loads, *loads):
        c.start()

    def copy(src, dst, sems, send_at, recv_at, to):
        return pltpu.make_async_remote_copy(
            src_ref=src, dst_ref=dst, send_sem=sems.at[(0, *send_at)], recv_sem=sems.at[(1, *recv_at)],
            device_id=to, device_id_type=MESH,
        )

    started = []

    def send(*args):
        c = copy(*args)
        c.start()
        started.append(c)

    def arrive(dst, sems, recv_at):
        copy(dst, dst, sems, recv_at, recv_at, other).wait_recv()

    for c in row_loads:
        c.wait()

    def folded(s):
        v = rows_in[s].astype(F32)
        return jnp.concatenate([v[:, 384 * c : 384 * (c + 1)] for c in range(4)], axis=0).astype(BF16)

    pieces[core, y, z] = folded(core)
    lent[...] = folded(1 - core)
    pl.semaphore_wait(barrier, len(everyone))

    send(lent, pieces.at[core, y, z], cx, (), (), other)
    for a in range(2):
        mine = pieces.at[a, y, z]

        @pl.when(core != a)
        def _():
            arrive(mine, cx, ())

        send(mine, mine, az, (a, jump), (a, z), over)
        for p, d in zip(near_z, along_z, strict=True):
            send(mine, mine, az, (a, p), (a, z), d)
    for i, ref in enumerate((w_up_ref, w_down_ref)):
        send(ref, weights.at[i, core], wx, (i,), (i,), other)

    def crossed(p):
        return 4 * (1 - half) + p % 4

    def pass_on(a):
        block = pieces.at[a, y, jump]
        arrive(block, az, (a, jump))
        for p, d in zip(near_z, along_z, strict=True):
            send(block, block, az, (a, crossed(p)), (a, jump), d)

    def part_of(k, q):
        return pieces.at[k // 2, q, pl.ds(4 * (half if k % 2 == 0 else 1 - half), 4)]

    def over_y(k):
        a = k // 2
        for p in near_z:
            p = p if k % 2 == 0 else crossed(p)
            arrive(pieces.at[a, y, p], az, (a, p))
        block = part_of(k, y)
        for p, d in zip(y_peers, along_y, strict=True):
            send(block, block, ay, (k, p), (k, y), d)

    top = lax.broadcasted_iota(jnp.int32, (2, 8, 384), 1) < 4

    def order(k, q):
        v = part_of(k, q)[...].astype(F32).reshape(2, 2, 2, 8, 384)
        rows = pl.ds(pl.multiple_of(16 * q, 16), 16)
        for c in range(4):
            first, second = v[:, 0, c // 2], v[:, 1, c // 2]
            if c % 2 == 0:
                block = jnp.where(top, first, pltpu.roll(second, 4, 1))
            else:
                block = jnp.where(top, pltpu.roll(first, 4, 1), second)
            full[core, k, rows, 384 * c : 384 * (c + 1)] = block.reshape(16, 384).astype(BF16)

    def project(h):
        pair = (h, 2 + h)
        for k in pair:
            order(k, y)
            for p in y_order:
                arrive(part_of(k, p), ay, (k, p))
                order(k, p)
        if h == 0:
            for i in range(2):
                loads[i].wait()
                arrive(weights.at[i, 1 - core], wx, (i,))
        rows = jnp.concatenate([full[core, k] for k in pair], axis=0)
        for f in range(2):
            sums = along_rows(rows, weights[core, f]).astype(BF16).reshape(2, NX, 16, 384)
            for n, k in enumerate(pair):
                part[k, :, f] = sums[n]
        for k in pair:
            for p, d in zip(x_peers, along_x, strict=True):
                send(part.at[k, p], xin.at[k, x], xr, (k, p), (k, x), d)
        for k in pair:
            send(full.at[core, k], full.at[core, k], fx, (k,), (k,), other)

    def to_far(a):
        total = part[a, x].astype(F32)
        for p in x_order:
            arrive(xin.at[a, p], xr, (a, p))
            total += xin[a, p].astype(F32)
        far_out[a] = total.astype(BF16)
        send(far_out.at[a], far_in.at[a], fz, (a,), (a,), far)

    def slope_copy(a):
        return copy(slopes_out.at[a], slopes.at[a], sx, (a,), (a,), other)

    def activate(a):
        arrive(far_in.at[a], fz, (a,))

        @pl.when(core == 0)
        def _():
            pre = far_out[a].astype(F32) + far_in[a].astype(F32)
            slopes_out[a] = gelu_slope(pre)
            slope_copy(a).start()
            hidden[core, a, x] = gelu_value(pre).astype(BF16)

        @pl.when(core == 1)
        def _():
            slope_copy(a).wait_recv()
            grad_act = far_out[a].astype(F32) + far_in[a].astype(F32)
            hidden[core, a, x] = (grad_act * slopes[a]).astype(BF16)

        block = hidden.at[core, a, x]
        for p, d in zip(x_peers, along_x, strict=True):
            send(block, block, xa, (a, p), (a, x), d)

    def back(a):
        for p in x_order:
            arrive(hidden.at[core, a, p], xa, (a, p))
        for n in range(2):
            cols = slice(768 * n, 768 * (n + 1))
            total = sum(
                jnp.dot(
                    hidden[core, a, :, f].reshape(64, 384), weights[1 - core, f, :, cols], preferred_element_type=F32
                )
                for f in range(2)
            )
            y_out[a, :, :, cols] = total.astype(BF16).reshape(NY, 16, 768)
        for p, d in zip(y_peers, along_y, strict=True):
            send(y_out.at[a, p], y_in.at[a, y], ry, (a, p), (a, y), d)
        lend = hidden.at[core, a, :, 1 - core]
        send(lend, lend, hx, (a,), (a,), other)

    def to_z(k):
        total = y_out[k, y].astype(F32)
        for p in y_order:
            arrive(y_in.at[k, p], ry, (k, p))
            total += y_in[k, p].astype(F32)
        rows = total.reshape(2, 8, 1536)
        c = [rows[:, :, 384 * i : 384 * (i + 1)] for i in range(4)]
        for parity in range(2):
            tiles = [
                jnp.where(top, c[2 * r], pltpu.roll(c[2 * r + 1], 4, 1))
                if parity == 0
                else jnp.where(top, pltpu.roll(c[2 * r], 4, 1), c[2 * r + 1])
                for r in range(2)
            ]
            z_out[k, :, parity] = jnp.concatenate(tiles, axis=1).astype(BF16)
        mine = z % 4
        for p, d in zip(near_z, along_z, strict=True):
            send(z_out.at[k, p % 4 // 2, p % 2], z_in.at[k, mine], rz, (k, p % 4), (k, mine), d)
        z_in[k, mine] = z_out[k, mine // 2, mine % 2]

    def half_sum(k):
        for p in near_z:
            arrive(z_in.at[k, p % 4], rz, (k, p % 4))
        return sum(z_in[k, i].astype(F32) for i in range(4))

    def cross(a):
        jump_out[a] = half_sum(2 * a + 1).astype(BF16)
        send(jump_out.at[a], jump_in.at[a], rj, (a,), (a,), over)

    def unfolded(v):
        low, high = v[:8], v[8:]
        return jnp.concatenate([low, pltpu.roll(low, 4, 0), high, pltpu.roll(high, 4, 0)], axis=1)[:4]

    last_copy = copy(last_out, last_in, lx, (), (), other)

    def finish(a, own_ref):
        total = half_sum(2 * a)
        arrive(jump_in.at[a], rj, (a,))
        total += jump_in[a].astype(F32)

        @pl.when(core == a)
        def _():
            own_ref[...] = unfolded(total).astype(BF16)

        @pl.when(core != a)
        def _():
            last_out[...] = total.astype(BF16)
            last_copy.start()

    def weight_grad(s, ref):
        h = hidden[1 - s, :, :, core].reshape(256, 384)
        for c in range(4):
            cols = slice(384 * c, 384 * (c + 1))
            ref[:, cols] = (over_tokens(h, full[s, :, :, cols].reshape(256, 384)) * scale).astype(BF16)

    over_y(0)
    pass_on(0)
    over_y(2)
    pass_on(1)
    over_y(1)
    over_y(3)
    project(0)
    project(1)
    to_far(0)
    to_far(2)
    to_far(1)
    to_far(3)
    activate(0)
    activate(2)
    back(0)
    activate(1)
    back(2)
    activate(3)
    back(1)
    to_z(0)
    back(3)
    to_z(2)
    to_z(1)
    for k in range(4):
        arrive(full.at[1 - core, k], fx, (k,))
        arrive(hidden.at[1 - core, k, :, core], hx, (k,))
    weight_grad(0, gwu_ref)
    to_z(3)
    cross(0)
    cross(1)
    weight_grad(1, gwd_ref)
    finish(0, out_ref)
    finish(1, gin_ref)
    last_copy.wait()
    theirs = unfolded(last_in[...].astype(F32)).astype(BF16)

    @pl.when(core == 0)
    def _():
        gin_ref[...] = theirs
        for k in range(4):
            slope_copy(k).wait_send()

    @pl.when(core == 1)
    def _():
        out_ref[...] = theirs

    for c in started:
        c.wait_send()


def write_out(*refs):
    sources, targets, sem = refs[:4], refs[4:8], refs[8]
    copies = [pltpu.make_async_copy(a, b, sem.at[i]) for i, (a, b) in enumerate(zip(sources, targets, strict=True))]
    for c in copies:
        c.start()
    for c in copies:
        c.wait()


def local(tokens, w_up, w_down, grad_out):
    n_tokens = tokens.shape[0] * lax.axis_size("depth") * lax.axis_size("row")
    scale = 1.0 / math.sqrt(n_tokens)
    vmem, hbm = pl.BlockSpec(memory_space=pltpu.VMEM), pl.BlockSpec(memory_space=pltpu.HBM)
    dma = pltpu.SemaphoreType.DMA
    shape = jax.ShapeDtypeStruct
    shapes = (
        shape((4, 1536), BF16), shape((4, 1536), BF16), shape((384, 1536), BF16), shape((384, 1536), BF16),
    )
    held = pltpu.with_memory_space_constraint
    results = pl.pallas_call(
        functools.partial(kernel, scale),
        name="ffn",
        out_shape=tuple(pltpu.VMEM(a.shape, a.dtype) for a in shapes),
        in_specs=[hbm] * 4,
        out_specs=(vmem,) * 4,
        scratch_shapes=[
            pltpu.VMEM((2, 4, 1536), BF16),
            pltpu.VMEM((2, 2, 384, 1536), BF16),
            pltpu.VMEM((16, 384), BF16),
            pltpu.VMEM((2, NY, NZ, 16, 384), BF16),
            pltpu.VMEM((2, 4, 64, 1536), BF16),
            pltpu.VMEM((4, NX, 2, 16, 384), BF16),
            pltpu.VMEM((4, NX, 2, 16, 384), BF16),
            pltpu.VMEM((4, 2, 16, 384), BF16),
            pltpu.VMEM((4, 2, 16, 384), BF16),
            pltpu.VMEM((4, 2, 16, 384), F32),
            pltpu.VMEM((4, 2, 16, 384), F32),
            pltpu.VMEM((2, 4, NX, 2, 16, 384), BF16),
            pltpu.VMEM((4, NY, 16, 1536), BF16),
            pltpu.VMEM((4, NY, 16, 1536), BF16),
            pltpu.VMEM((4, 2, 2, 16, 384), BF16),
            pltpu.VMEM((4, 4, 16, 384), BF16),
            pltpu.VMEM((2, 16, 384), BF16),
            pltpu.VMEM((2, 16, 384), BF16),
            pltpu.VMEM((16, 384), BF16),
            pltpu.VMEM((16, 384), BF16),
            dma((2,)), dma((2,)), dma((2, 2)), dma((2,)),
            dma((2, 2, NZ)), dma((2, 4, NY)), dma((2, 4)), dma((2, 4, NX)), dma((2, 4)), dma((2, 4)), dma((2, 4, NX)),
            dma((2, 4)), dma((2, 4, NY)), dma((2, 4, 4)), dma((2, 2)), dma((2,)),
        ],
        compiler_params=pltpu.CompilerParams(
            collective_id=0, has_side_effects=True, vmem_limit_bytes=48 << 20
        ),
    )(*(held(a, pltpu.HBM) for a in (tokens, w_up, w_down, grad_out)))
    return pl.pallas_call(
        write_out,
        name="write_out",
        out_shape=tuple(pltpu.HBM(a.shape, a.dtype) for a in shapes),
        in_specs=[vmem] * 4,
        out_specs=(hbm,) * 4,
        scratch_shapes=[dma((4,))],
    )(*(held(a, pltpu.VMEM) for a in results))


def solution(mesh):
    spec = P(("depth", "row"), "col")
    return jax.shard_map(
        local, mesh=mesh, in_specs=(spec,) * 4, out_specs=(spec,) * 4, check_vma=False
    )
```
